512 devices in a mesh: dp: 32 (over y_lo, z), tensor: 16 (over y_hi, x, core).
Axes of the slice: x: 4, y: 8 (y_hi: 2, y_lo: 4; y = y_hi * 4 + y_lo), z: 8, core: 2. Of those that a mesh axis runs over, the one named last changes fastest.
Arguments:
- hidden: bfloat16 [4096, 16384], P('dp', 'tensor'), may hold values from -6 to 6
- down_weight: bfloat16 [16384, 4096], P('tensor', 'dp'), may hold values from -0.046875 to 0.046875
- factor_a: bfloat16 [1024, 16384], P('dp', 'tensor'), may hold values from -0.046875 to 0.046875
- factor_b: bfloat16 [1024, 4096], P('dp', 'tensor'), may hold values from -0.375 to 0.375
- cotangent: bfloat16 [4096, 4096], P('dp', 'tensor'), may hold values from -6 to 6
- block_job: int32 [64, 1], P('dp'), may hold values from 0 to 3
- ranks: int32 [4], replicated, may hold values from 64 to 256, as said below
Outputs:
- mixed: bfloat16 [4096, 4096], P('dp', 'tensor')
- hidden_grad: bfloat16 [4096, 16384], P('dp', 'tensor')
- grad_a: bfloat16 [1024, 16384], P('dp', 'tensor')
- grad_b: bfloat16 [1024, 4096], P('dp', 'tensor')
The draws below stay inside these ranges and needn't reach their ends.
Inputs may be any that keep to these rules, and one draw needn't show every extreme that they name: `ranks`: every job uses a multiple of 64 rank slots, and each multiple from 64 to 256 is used by one job.
All inputs are finite; a program needn't handle non-finite values.
Results may differ from the reference program's by a relative error of at most 0.022.
Values may be sent and summed in bfloat16 or wider, within the bound.
A program may use at most 64 MiB of HBM per device.

```python
import jax
import jax.numpy as jnp
from jax import lax

DW = 4096
FFW = 16384
R = 256
JOBS = 4
BLOCK = 64
TOK_DEV = 128
TOKENS = 4096
NBLOCKS = 64
N_DP = 32
N_TENSOR = 16


def draw_ranks(key, part):
    key = jax.random.fold_in(key, 7)
    order = jax.random.permutation(key, JOBS)
    return ((order % 4 + 1) * (R // 4)).astype(jnp.int32)


def levels(rng, dims, cuts, low, top_value):
    factor_of = 1.0
    for axis_at, shards_of in cuts:
        steps = jax.random.uniform(jax.random.fold_in(jax.random.fold_in(rng, 6), axis_at), (shards_of,), jnp.float32, low / len(cuts), top_value / len(cuts))
        factor_of = factor_of * jnp.repeat(jnp.exp(steps), dims[axis_at] // shards_of).reshape((-1,) + (1,) * (len(dims) - 1 - axis_at))
    return factor_of


def different_ones(stream_key, rows, number_of, top, lift):
    sequence = jax.random.permutation(jax.random.fold_in(stream_key, 1), number_of)
    favour = sequence
    for power in range(3):
        favour = favour * favour // number_of
    favour = favour * lift // number_of
    lots = jax.random.randint(jax.random.fold_in(stream_key, 2), (rows, number_of), 0, 4096) + favour
    holders = jax.random.permutation(jax.random.fold_in(stream_key, 3), rows)[jnp.arange(number_of) % rows]
    lots = jnp.where(jnp.arange(rows)[:, None] == holders[None, :], 1 << 14, lots)
    priority = lots * number_of + jnp.arange(number_of)
    return lax.top_k(priority.astype(jnp.int32), top)[1].astype(jnp.int32)


def gaussian(stream_key, shape, width, most, split=(), held_as=jnp.bfloat16):
    factor_of = levels(stream_key, shape, split, -0.22, 0.18) if split else 1.0
    entries = jax.random.normal(stream_key, shape, jnp.float32) * width * factor_of
    return jnp.minimum(jnp.maximum(entries, -most), most).astype(held_as)


def setup_inputs(seed: int = 0) -> dict:
    streams_of = jax.random.split(jax.random.key(seed), 8)
    return {
        "hidden": gaussian(streams_of[0], (TOKENS, FFW), 1.0, 6.0, ((0, 32), (1, 16))),
        "down_weight": gaussian(streams_of[1], (FFW, DW), FFW ** -0.5, 0.046875, ((0, 16), (1, 32))),
        "factor_a": gaussian(streams_of[2], (JOBS * R, FFW), FFW ** -0.5, 0.046875, ((0, 32), (1, 16))),
        "factor_b": gaussian(streams_of[3], (JOBS * R, DW), R ** -0.5, 0.375, ((0, 32), (1, 16))),
        "cotangent": gaussian(streams_of[4], (TOKENS, DW), 1.0, 6.0, ((0, 32), (1, 16))),
        "block_job": different_ones(streams_of[5], NBLOCKS, JOBS, 1, 4096),
        "ranks": draw_ranks(jax.random.fold_in(streams_of[7], 71), 0),
    }


adapter_scale = 2.0


def build_mask(block_job, ranks):
    token_job = jnp.repeat(block_job[:, 0], BLOCK)
    job_index = jnp.arange(JOBS, dtype=jnp.int32)
    onehot = token_job[:, None] == job_index[None, :]
    token_rank = jnp.sum(jnp.where(onehot, ranks[None, :], 0), axis=1)
    column = jnp.arange(JOBS * R, dtype=jnp.int32)
    keep = (column[None, :] // R == token_job[:, None]) & (column[None, :] % R < token_rank[:, None])
    return keep.astype(jnp.float32)


def rounded_sum(first, second):
    def step_one(total, pair):
        term = jnp.dot(pair[0], pair[1], preferred_element_type=jnp.float32).astype(jnp.bfloat16)
        term = lax.optimization_barrier(term)
        return total + term.astype(jnp.float32), None
    start = jnp.zeros((first.shape[1], second.shape[2]), jnp.float32)
    total, unused = lax.scan(step_one, start, (first, second))
    return total


def reference(hidden, down_weight, factor_a, factor_b, cotangent, block_job, ranks):
    keep_mask = build_mask(block_job, ranks)
    delta = keep_mask * jnp.dot(hidden, factor_a.T, preferred_element_type=jnp.float32)
    delta_low = delta.astype(jnp.bfloat16)
    ff_piece = FFW // N_TENSOR
    hidden_groups = hidden.reshape(TOKENS, N_TENSOR, ff_piece).transpose(1, 0, 2)
    weight_groups = down_weight.reshape(N_TENSOR, ff_piece, DW)
    frozen = rounded_sum(hidden_groups, weight_groups)
    mixed = (frozen + adapter_scale * jnp.dot(delta_low, factor_b, preferred_element_type=jnp.float32)).astype(jnp.bfloat16)
    grad_delta = keep_mask * jnp.dot(cotangent, factor_b.T, preferred_element_type=jnp.float32)
    grad_low = grad_delta.astype(jnp.bfloat16)
    hidden_grad = (jnp.dot(cotangent, down_weight.T, preferred_element_type=jnp.float32)
                   + adapter_scale * jnp.dot(grad_low, factor_a, preferred_element_type=jnp.float32)).astype(jnp.bfloat16)
    scaled_grad = (grad_low.astype(jnp.float32) * adapter_scale).reshape(N_DP, TOK_DEV, JOBS * R).transpose(0, 2, 1)
    scaled_delta = (delta_low.astype(jnp.float32) * adapter_scale).reshape(N_DP, TOK_DEV, JOBS * R).transpose(0, 2, 1)
    hidden_tok = hidden.astype(jnp.float32).reshape(N_DP, TOK_DEV, FFW)
    cot_tok = cotangent.astype(jnp.float32).reshape(N_DP, TOK_DEV, DW)
    grad_a = rounded_sum(scaled_grad, hidden_tok).astype(jnp.bfloat16)
    grad_b = rounded_sum(scaled_delta, cot_tok).astype(jnp.bfloat16)
    return mixed, hidden_grad, grad_a, grad_b
```

```python
import jax
import jax.numpy as jnp
from jax import lax
from jax.experimental import pallas as pl
from jax.experimental.pallas import tpu as pltpu
from jax.sharding import PartitionSpec as P

R = 256
JOBS = 4
BLOCK = 64
NYL, NZ, NX = 4, 8, 4

BF = jnp.bfloat16
F32 = jnp.float32
MESH = pl.DeviceIdType.MESH
NN = (((1,), (0,)), ((), ()))
NT = (((1,), (1,)), ((), ()))
TN = (((0,), (0,)), ((), ()))

adapter_scale = 2.0


def dot(first, second, dims=NN):
    return lax.dot_general(first, second, dims, preferred_element_type=F32)


def loop(count, body, start=1):
    def step(k, carry):
        body(k)
        return carry

    lax.fori_loop(start, start + count, step, 0)


class Sends:
    def __init__(self, sems, base, out, into):
        self.send, self.recv = sems
        self.base, self.out, self.into = base, out, into

    def copy(self, k):
        src, dst, dev = self.out(k)
        return pltpu.make_async_remote_copy(
            src_ref=src,
            dst_ref=dst,
            send_sem=self.send.at[self.base + k],
            recv_sem=self.recv.at[self.base + k],
            device_id=dev,
            device_id_type=MESH,
        )

    def start(self, k):
        self.copy(k).start()

    def landed(self, k):
        src, dst, dev = self.out(k)
        pltpu.make_async_remote_copy(
            src_ref=src,
            dst_ref=self.into(k),
            send_sem=self.send.at[self.base + k],
            recv_sem=self.recv.at[self.base + k],
            device_id=dev,
            device_id_type=MESH,
        ).wait_recv()

    def left(self, k):
        self.copy(k).wait_send()


def kernel(
    hid, w, a, b, cot, lim,
    mixed_o, hg_o, ga_o, gb_o,
    hid_g, w_g, a_g, b_g, cot_g, lim_g, cr,
    part, part_in, tot, yh_out, yh_in, low,
    hg_src, hg_dst, ga_src, ga_dst, gb_src, gb_dst, ml_src, ml_dst,
    fc_src, fc_dst, fx_src, fx_dst, ff_src, ff_dst,
    send_sem, recv_sem,
):
    d = lax.axis_index("dp")
    t = lax.axis_index("tensor")
    yl, z = lax.div(d, 8), lax.rem(d, 8)
    yh, o = lax.div(t, 8), lax.rem(t, 8)
    x, c = lax.div(o, 2), lax.rem(o, 2)

    def yl_at(k):
        return lax.rem(yl + k + 4, 4)

    def z_at(k):
        return lax.rem(z + k + 16, 8)

    def o_at(k):
        return lax.rem(o + k + 8, 8)

    def x_at(k):
        return lax.rem(x + k + 4, 4)

    def yl_peer(k):
        return (yl_at(k) * 8 + z, t)

    def z_peer(k):
        return (yl * 8 + z_at(k), t)

    def o_peer(k):
        return (d, yh * 8 + o_at(k))

    def x_peer(k):
        return (d, yh * 8 + x_at(k) * 2 + c)

    sibling = (d, t + 1 - 2 * c)
    partner = (d, lax.rem(t + 8, 16))

    last_dp = x * 8 + z

    def last_t(xb):
        return lax.div(yl, 2) * 8 + (lax.rem(yl, 2) * 2 + xb) * 2 + c

    def last_here(xb):
        return jnp.logical_and(last_dp == d, last_t(xb) == t)

    first_dp = (2 * yh + lax.div(x, 2)) * 8 + z

    def first_t(h):
        return h * 8 + yl * 2 + c

    def first_here(h):
        return jnp.logical_and(first_dp == d, first_t(h) == t)

    sems = (send_sem, recv_sem)
    bases = [0]

    def family(count, out, into):
        base = bases[0]
        bases[0] += count
        return Sends(sems, base, out, into)

    s_cot = family(4, lambda k: (cot_g.at[yl], cot_g.at[yl], yl_peer(k)), lambda k: cot_g.at[yl_at(-k)])
    s_lim = family(4, lambda k: (lim.at[yl_at(k)], lim_g.at[yl], yl_peer(k)), lambda k: lim_g.at[yl_at(-k)])
    s_hid = family(4, lambda k: (hid_g.at[yl], hid_g.at[yl], yl_peer(k)), lambda k: hid_g.at[yl_at(-k)])
    s_b = family(8, lambda k: (b_g.at[z], b_g.at[z], z_peer(k)), lambda k: b_g.at[z_at(-k)])
    turn = 1 - 2 * c
    rings = []
    for buf in (a_g, w_g):
        right = family(
            4,
            lambda s, buf=buf: (buf.at[z_at(1 - s)], buf.at[z_at(1 - s)], z_peer(1)),
            lambda s, buf=buf: buf.at[z_at(-s)],
        )
        left = family(
            4,
            lambda s, buf=buf: (buf.at[z_at(s - 1)], buf.at[z_at(s - 1)], z_peer(-1)),
            lambda s, buf=buf: buf.at[z_at(s)],
        )
        across = family(
            1,
            lambda s, buf=buf: (buf.at[z_at(-3 * turn)], buf.at[z_at(-3 * turn)], z_peer(turn)),
            lambda s, buf=buf: buf.at[z_at(4)],
        )
        rings.append((right, left, across))

    def ring_start(s):
        for right, left, across in rings:
            if s < 4:
                right.start(s)
                left.start(s)
            else:
                across.start(0)

    def ring_landed(s):
        for right, left, across in rings:
            if s < 4:
                right.landed(s)
                left.landed(s)
            else:
                across.landed(0)

    s_part, s_yh, s_low = [], [], []
    for i in range(2):
        s_part.append(
            family(8, lambda k, i=i: (part.at[i, o_at(k)], part_in.at[i, k], o_peer(k)), lambda k, i=i: part_in.at[i, k])
        )
        s_yh.append(family(1, lambda k, i=i: (yh_out.at[i], yh_in.at[i], partner), lambda k, i=i: yh_in.at[i]))
        s_low.append(
            family(8, lambda k, i=i: (low.at[i, o], low.at[i, o], o_peer(k)), lambda k, i=i: low.at[i, o_at(-k)])
        )

    xb_me = lax.rem(x, 2)
    is_root = lax.div(x, 2) == lax.rem(yl, 2)
    is_native = yh == lax.div(yl, 2)
    native_root = jnp.logical_and(is_root, is_native)
    far_root = jnp.logical_and(is_root, jnp.logical_not(is_native))
    mine = xb_me * 2 + c
    s_cry = family(1, lambda k: (cr.at[mine], cr.at[mine], partner), lambda k: cr.at[mine])
    crx_base = bases[0]
    bases[0] += 4
    crx_recv = bases[0]
    bases[0] += 2

    def crx(k, xb):
        return pltpu.make_async_remote_copy(
            src_ref=cr.at[mine],
            dst_ref=cr.at[xb * 2 + c],
            send_sem=send_sem.at[crx_base + k],
            recv_sem=recv_sem.at[crx_recv + xb],
            device_id=x_peer(k),
            device_id_type=MESH,
        )

    s_crc = family(2, lambda xb: (cr.at[xb * 2 + c], cr.at[xb * 2 + c], sibling), lambda xb: cr.at[xb * 2 + 1 - c])

    hg_base = bases[0]
    bases[0] += 16
    s_hg = [
        Sends(
            sems,
            hg_base + 4 * n,
            lambda k, n=n: (hg_src.at[n, yl_at(k)], hg_dst.at[n, k], yl_peer(k)),
            lambda k, n=n: hg_dst.at[n, k],
        )
        for n in range(4)
    ]
    s_ga = family(8, lambda k: (ga_src.at[z_at(k)], ga_dst.at[k], z_peer(k)), lambda k: ga_dst.at[k])
    s_gb = family(8, lambda k: (gb_src.at[z_at(k)], gb_dst.at[k], z_peer(k)), lambda k: gb_dst.at[k])
    s_ml = family(4, lambda k: (ml_src.at[yl_at(k)], ml_dst.at[k], yl_peer(k)), lambda k: ml_dst.at[k])
    s_fc = family(2, lambda xb: (fc_src.at[xb], fc_dst.at[xb], sibling), lambda xb: fc_dst.at[xb])
    s_fx = family(4, lambda k: (fx_src.at[x_at(k)], fx_dst.at[k], x_peer(k)), lambda k: fx_dst.at[k])
    ff_send = bases[0]
    bases[0] += 2

    def ff(xb, h):
        return pltpu.make_async_remote_copy(
            src_ref=ff_src.at[xb],
            dst_ref=ff_dst.at[h],
            send_sem=send_sem.at[ff_send + xb],
            recv_sem=recv_sem.at[ff_send + h],
            device_id=(last_dp, last_t(xb)),
            device_id_type=MESH,
        )

    cot_g[yl] = cot[...]
    lim_g[yl] = lim[yl]
    b_g[z] = b[...]
    a_g[z] = a[...]
    w_g[z] = w[...]
    hid_g[yl] = hid[...]

    barrier = pltpu.get_barrier_semaphore()

    def greet(dev):
        pl.semaphore_signal(barrier, inc=1, device_id=dev, device_id_type=MESH)

    loop(3, lambda k: greet(yl_peer(k)))
    loop(7, lambda k: greet(z_peer(k)))
    loop(7, lambda k: greet(o_peer(k)))
    greet(partner)
    for xb in range(2):
        @pl.when(jnp.logical_not(last_here(xb)))
        def _(xb=xb):
            greet((last_dp, last_t(xb)))

        @pl.when(jnp.logical_not(first_here(xb)))
        def _(xb=xb):
            greet((first_dp, first_t(xb)))

    own_last = jnp.logical_or(last_here(0), last_here(1)).astype(jnp.int32)
    pl.semaphore_wait(barrier, 22 - 2 * own_last)

    loop(3, s_cot.start)
    loop(3, s_lim.start)
    loop(7, s_b.start)
    ring_start(1)
    loop(3, s_cot.landed)
    loop(3, s_lim.landed)

    @pl.when(native_root)
    def _():
        cr[mine] = cot_g[...].reshape(512, 256)
        s_cry.start(0)
        loop(3, lambda k: crx(k, xb_me).start())

    loop(3, s_hid.start)
    loop(7, s_b.landed)

    def partial(i, value):
        part[i] = value.astype(BF).reshape(8, 64, 256)
        loop(7, s_part[i].start)

    def halfway(i):
        loop(7, s_part[i].landed)
        value = part[i, o].astype(F32)
        for k in range(1, 8):
            value = value + part_in[i, k].astype(F32)
        limit = lim_g[x, pl.ds(pl.multiple_of(c * 8, 8), 8), :][0:1, :]
        limit = jnp.concatenate([limit, limit], axis=1)
        column = lax.broadcasted_iota(jnp.int32, (64, 256), 1).astype(F32)
        value = jnp.where(column < limit, value, 0.0)
        tot[i] = value
        yh_out[i] = value.astype(BF)
        s_yh[i].start(0)

    def whole(i):
        s_yh[i].landed(0)
        low[i, o] = (tot[i] + yh_in[i].astype(F32)).astype(BF)
        loop(7, s_low[i].start)

    factor_b = b_g[...].reshape(256, 256)
    partial(0, dot(cot_g[...].reshape(512, 256), factor_b, NT))

    ring_landed(1)
    ring_start(2)
    halfway(0)

    @pl.when(far_root)
    def _():
        s_cry.landed(0)
        loop(3, lambda k: crx(k, xb_me).start())

    ring_landed(2)
    ring_start(3)
    whole(0)

    for xb in range(2):
        @pl.when(x != lax.rem(yl, 2) * 2 + xb)
        def _(xb=xb):
            crx(1, xb).wait_recv()

        s_crc.start(xb)

    ring_landed(3)
    ring_start(4)

    loop(7, s_low[0].landed)
    for xb in range(2):
        s_crc.landed(xb)
    ring_landed(4)

    def hg_tile(n, send):
        rows = pl.ds(pl.multiple_of(n * 256, 256), 256)
        acc = adapter_scale * dot(low[0].reshape(512, 256), a_g[:, :, rows].reshape(256, 256))
        for j in range(4):
            pair = jnp.concatenate([w_g[2 * j, rows, :], w_g[2 * j + 1, rows, :]], axis=1)
            acc = acc + dot(cr[j], pair, NT)
        hg_src[n] = acc.astype(BF).reshape(4, 128, 256)
        loop(3, send)

    for n in range(4):
        hg_tile(n, s_hg[n].start)

    loop(3, s_hid.landed)
    partial(1, dot(hid_g[...].reshape(512, 1024), a_g[...].reshape(256, 1024), NT))

    def frozen(xb, cc):
        j = xb * 2 + cc
        pair = jnp.concatenate([w_g[2 * j], w_g[2 * j + 1]], axis=1)
        return dot(hid_g[...].reshape(512, 1024), pair)

    for xb in range(2):
        fc_src[xb] = frozen(xb, 1 - c).astype(BF)
        s_fc.start(xb)

    halfway(1)

    def ga_tile(n):
        cols = pl.ds(pl.multiple_of(n * 256, 256), 256)
        term = adapter_scale * dot(low[0].reshape(512, 256), hid_g[:, :, cols].reshape(512, 256), TN)
        ga_src[:, :, cols] = term.astype(BF).reshape(8, 32, 256)

    loop(4, ga_tile, 0)
    loop(7, s_ga.start)
    whole(1)

    for xb in range(2):
        acc = frozen(xb, c)
        s_fc.landed(xb)
        acc = acc + fc_dst[xb].astype(F32)
        fx_src[:, xb] = acc.astype(BF).reshape(4, 128, 256)
    loop(3, s_fx.start)

    loop(7, s_low[1].landed)
    ml_src[...] = (adapter_scale * dot(low[1].reshape(512, 256), factor_b)).astype(BF).reshape(4, 128, 256)
    loop(3, s_ml.start)
    gb_src[...] = (
        adapter_scale * dot(low[1].reshape(512, 256), cot_g[...].reshape(512, 256), TN)
    ).astype(BF).reshape(8, 32, 256)
    loop(7, s_gb.start)

    loop(3, s_fx.landed)
    value = fx_src[x].astype(F32)
    for k in range(1, 4):
        value = value + fx_dst[k].astype(F32)
    ff_src[...] = value.astype(BF)
    for xb in range(2):
        @pl.when(last_here(xb))
        def _(xb=xb):
            ff_dst[yh] = ff_src[xb]

        @pl.when(jnp.logical_not(last_here(xb)))
        def _(xb=xb):
            ff(xb, yh).start()

    for n in range(4):
        loop(3, s_hg[n].landed)
        value = hg_src[n, yl].astype(F32)
        for k in range(1, 4):
            value = value + hg_dst[n, k].astype(F32)
        hg_o[:, 256 * n : 256 * (n + 1)] = value.astype(BF)

    loop(7, s_ga.landed)
    value = ga_src[z].astype(F32)
    for k in range(1, 8):
        value = value + ga_dst[k].astype(F32)
    ga_o[...] = value.astype(BF)

    loop(7, s_gb.landed)
    value = gb_src[z].astype(F32)
    for k in range(1, 8):
        value = value + gb_dst[k].astype(F32)
    gb_o[...] = value.astype(BF)

    loop(3, s_ml.landed)
    for h in range(2):
        @pl.when(jnp.logical_not(first_here(h)))
        def _(h=h):
            ff(0, h).wait_recv()

    value = ff_dst[0].astype(F32) + ff_dst[1].astype(F32) + ml_src[yl].astype(F32)
    for k in range(1, 4):
        value = value + ml_dst[k].astype(F32)
    mixed_o[...] = value.astype(BF)

    for family_of in (s_cot, s_lim, s_hid, s_ml, s_fx, *s_hg):
        loop(3, family_of.left)
    for family_of in (s_b, *s_part, *s_low, s_ga, s_gb):
        loop(7, family_of.left)
    for right, left, across in rings:
        loop(3, right.left)
        loop(3, left.left)
        across.left(0)
    for family_of in s_yh:
        family_of.left(0)
    for xb in range(2):
        s_crc.left(xb)
        s_fc.left(xb)

        @pl.when(jnp.logical_not(last_here(xb)))
        def _(xb=xb):
            ff(xb, yh).wait_send()

    @pl.when(native_root)
    def _():
        s_cry.left(0)

    @pl.when(is_root)
    def _():
        loop(3, lambda k: crx(k, xb_me).wait_send())


SEMS = 192


def on_device(hidden, down_weight, factor_a, factor_b, cotangent, block_job, ranks):
    jobs = jnp.arange(JOBS, dtype=jnp.int32)
    limit = jnp.where(block_job[:, 0][None, :] == jobs[:, None], ranks[:, None], 0)
    limit = jnp.repeat(limit, 8, axis=1).astype(F32)
    limit = jnp.broadcast_to(limit[:, :, None], (JOBS, 16, 128))

    def vmem(*shape, dtype=BF):
        return pltpu.VMEM(shape, dtype)

    shapes = ((128, 256), (128, 1024), (32, 1024), (32, 256))
    return pl.pallas_call(
        kernel,
        out_shape=tuple(jax.ShapeDtypeStruct(s, BF) for s in shapes),
        in_specs=[pl.BlockSpec(memory_space=pltpu.VMEM)] * 6,
        out_specs=tuple(pl.BlockSpec(memory_space=pltpu.VMEM) for s in shapes),
        scratch_shapes=[
            vmem(4, 128, 1024), vmem(8, 1024, 128), vmem(8, 32, 1024), vmem(8, 32, 256),
            vmem(4, 128, 256), vmem(4, 16, 128, dtype=F32), vmem(4, 512, 256),
            vmem(2, 8, 64, 256), vmem(2, 8, 64, 256), vmem(2, 64, 256, dtype=F32),
            vmem(2, 64, 256), vmem(2, 64, 256), vmem(2, 8, 64, 256),
            vmem(4, 4, 128, 256), vmem(4, 4, 128, 256), vmem(8, 32, 1024), vmem(8, 32, 1024),
            vmem(8, 32, 256), vmem(8, 32, 256), vmem(4, 128, 256), vmem(4, 128, 256),
            vmem(2, 512, 256), vmem(2, 512, 256), vmem(4, 2, 128, 256), vmem(4, 2, 128, 256),
            vmem(2, 128, 256), vmem(2, 128, 256),
            pltpu.SemaphoreType.DMA((SEMS,)), pltpu.SemaphoreType.DMA((SEMS,)),
        ],
        compiler_params=pltpu.CompilerParams(
            collective_id=0, has_side_effects=True, vmem_limit_bytes=48 * 1024 * 1024
        ),
        cost_estimate=pl.CostEstimate(flops=3_000_000_000, bytes_accessed=4_000_000, transcendentals=0),
    )(hidden, down_weight, factor_a, factor_b, cotangent, limit)


def solution(mesh):
    in_specs = (
        P("dp", "tensor"),
        P("tensor", "dp"),
        P("dp", "tensor"),
        P("dp", "tensor"),
        P("dp", "tensor"),
        P("dp", None),
        P(),
    )
    out_specs = (P("dp", "tensor"), P("dp", "tensor"), P("dp", "tensor"), P("dp", "tensor"))
    return jax.shard_map(
        on_device, mesh=mesh, in_specs=in_specs, out_specs=out_specs, check_vma=False
    )
```

```python
import jax
import jax.numpy as jnp
from jax import lax
from jax.experimental import pallas as pl
from jax.experimental.pallas import tpu as pltpu
from jax.sharding import PartitionSpec as P

R = 256
JOBS = 4
BLOCK = 64
NYL, NZ, NX = 4, 8, 4

BF = jnp.bfloat16
F32 = jnp.float32
MESH = pl.DeviceIdType.MESH
NN = (((1,), (0,)), ((), ()))
NT = (((1,), (1,)), ((), ()))
TN = (((0,), (0,)), ((), ()))

adapter_scale = 2.0


def dot(first, second, dims=NN):
    return lax.dot_general(first, second, dims, preferred_element_type=F32)


def loop(count, body, start=1):
    def step(k, carry):
        body(k)
        return carry

    lax.fori_loop(start, start + count, step, 0)


class Sends:
    def __init__(self, sems, base, out, into):
        self.send, self.recv = sems
        self.base, self.out, self.into = base, out, into

    def copy(self, k):
        src, dst, dev = self.out(k)
        return pltpu.make_async_remote_copy(
            src_ref=src,
            dst_ref=dst,
            send_sem=self.send.at[self.base + k],
            recv_sem=self.recv.at[self.base + k],
            device_id=dev,
            device_id_type=MESH,
        )

    def start(self, k):
        self.copy(k).start()

    def landed(self, k):
        src, dst, dev = self.out(k)
        pltpu.make_async_remote_copy(
            src_ref=src,
            dst_ref=self.into(k),
            send_sem=self.send.at[self.base + k],
            recv_sem=self.recv.at[self.base + k],
            device_id=dev,
            device_id_type=MESH,
        ).wait_recv()

    def left(self, k):
        self.copy(k).wait_send()


def kernel(
    hid, w, a, b, cot, block_job, ranks,
    mixed_o, hg_o, ga_o, gb_o,
    hid_g, w_g, a_g, b_g, cot_g, lim, lim_g, cr,
    part, part_in, tot, yh_out, yh_in, low,
    hg_src, hg_dst, ga_src, ga_dst, gb_src, gb_dst, ml_src, ml_dst,
    fc_src, fc_dst, fx_src, fx_dst, ff_src, ff_dst,
    own_sem, send_sem, recv_sem,
):
    d = lax.axis_index("dp")
    t = lax.axis_index("tensor")
    yl, z = lax.div(d, 8), lax.rem(d, 8)
    yh, o = lax.div(t, 8), lax.rem(t, 8)
    x, c = lax.div(o, 2), lax.rem(o, 2)

    def yl_at(k):
        return lax.rem(yl + k + 4, 4)

    def z_at(k):
        return lax.rem(z + k + 16, 8)

    def o_at(k):
        return lax.rem(o + k + 8, 8)

    def x_at(k):
        return lax.rem(x + k + 4, 4)

    def yl_peer(k):
        return (yl_at(k) * 8 + z, t)

    def z_peer(k):
        return (yl * 8 + z_at(k), t)

    def o_peer(k):
        return (d, yh * 8 + o_at(k))

    def x_peer(k):
        return (d, yh * 8 + x_at(k) * 2 + c)

    sibling = (d, t + 1 - 2 * c)
    partner = (d, lax.rem(t + 8, 16))

    last_dp = x * 8 + z

    def last_t(xb):
        return lax.div(yl, 2) * 8 + (lax.rem(yl, 2) * 2 + xb) * 2 + c

    def last_here(xb):
        return jnp.logical_and(last_dp == d, last_t(xb) == t)

    first_dp = (2 * yh + lax.div(x, 2)) * 8 + z

    def first_t(h):
        return h * 8 + yl * 2 + c

    def first_here(h):
        return jnp.logical_and(first_dp == d, first_t(h) == t)

    sems = (send_sem, recv_sem)
    bases = [0]

    def family(count, out, into):
        base = bases[0]
        bases[0] += count
        return Sends(sems, base, out, into)

    s_cot = family(4, lambda k: (cot_g.at[yl], cot_g.at[yl], yl_peer(k)), lambda k: cot_g.at[yl_at(-k)])
    s_lim = family(4, lambda k: (lim.at[yl_at(k)], lim_g.at[yl], yl_peer(k)), lambda k: lim_g.at[yl_at(-k)])
    s_hid = [
        family(
            4,
            lambda k, h=h: (hid_g.at[yl, h], hid_g.at[yl, h], yl_peer(k)),
            lambda k, h=h: hid_g.at[yl_at(-k), h],
        )
        for h in (pl.ds(0, 64), pl.ds(64, 64))
    ]
    s_b = family(8, lambda k: (b_g.at[z], b_g.at[z], z_peer(k)), lambda k: b_g.at[z_at(-k)])
    turn = 1 - 2 * c
    rings = []
    for at in (
        lambda slot: a_g.at[slot],
        lambda slot: w_g.at[slot, pl.ds(0, 512)],
        lambda slot: w_g.at[slot, pl.ds(512, 512)],
    ):
        right = family(
            4,
            lambda s, at=at: (at(z_at(1 - s)), at(z_at(1 - s)), z_peer(1)),
            lambda s, at=at: at(z_at(-s)),
        )
        left = family(
            4,
            lambda s, at=at: (at(z_at(s - 1)), at(z_at(s - 1)), z_peer(-1)),
            lambda s, at=at: at(z_at(s)),
        )
        across = family(
            1,
            lambda s, at=at: (at(z_at(-3 * turn)), at(z_at(-3 * turn)), z_peer(turn)),
            lambda s, at=at: at(z_at(4)),
        )
        rings.append((right, left, across))

    def ring_pass(s):
        for right, left, across in rings:
            if s == 4:
                across.landed(0)
                continue
            if s > 0:
                right.landed(s)
                left.landed(s)
            if s < 3:
                right.start(s + 1)
                left.start(s + 1)
            else:
                across.start(0)

    s_part, s_yh, s_low = [], [], []
    for i in range(2):
        s_part.append(
            family(8, lambda k, i=i: (part.at[i, o_at(k)], part_in.at[i, k], o_peer(k)), lambda k, i=i: part_in.at[i, k])
        )
        s_yh.append(family(1, lambda k, i=i: (yh_out.at[i], yh_in.at[i], partner), lambda k, i=i: yh_in.at[i]))
        s_low.append(
            family(8, lambda k, i=i: (low.at[i, o], low.at[i, o], o_peer(k)), lambda k, i=i: low.at[i, o_at(-k)])
        )

    xb_me = lax.rem(x, 2)
    is_root = lax.div(x, 2) == lax.rem(yl, 2)
    is_native = yh == lax.div(yl, 2)
    native_root = jnp.logical_and(is_root, is_native)
    far_root = jnp.logical_and(is_root, jnp.logical_not(is_native))
    mine = xb_me * 2 + c
    far_row = (2 * yh + lax.div(x, 2)) * 8 + z
    cry_base = bases[0]
    bases[0] += 4

    def cry(row):
        return pltpu.make_async_remote_copy(
            src_ref=cot_g.at[yl],
            dst_ref=cr.at[mine, row],
            send_sem=send_sem.at[cry_base],
            recv_sem=recv_sem.at[cry_base + row],
            device_id=(far_row, lax.rem(t + 8, 16)),
            device_id_type=MESH,
        )

    crx_base = bases[0]
    bases[0] += 4
    crx_recv = bases[0]
    bases[0] += 2

    def crx(k, xb):
        return pltpu.make_async_remote_copy(
            src_ref=cr.at[mine],
            dst_ref=cr.at[xb * 2 + c],
            send_sem=send_sem.at[crx_base + k],
            recv_sem=recv_sem.at[crx_recv + xb],
            device_id=x_peer(k),
            device_id_type=MESH,
        )

    s_crc = family(2, lambda xb: (cr.at[xb * 2 + c], cr.at[xb * 2 + c], sibling), lambda xb: cr.at[xb * 2 + 1 - c])

    hg_base = bases[0]
    bases[0] += 16
    s_hg = [
        Sends(
            sems,
            hg_base + 4 * n,
            lambda k, n=n: (hg_src.at[n, yl_at(k)], hg_dst.at[n, k], yl_peer(k)),
            lambda k, n=n: hg_dst.at[n, k],
        )
        for n in range(4)
    ]
    s_ga = family(8, lambda k: (ga_src.at[z_at(k)], ga_dst.at[k], z_peer(k)), lambda k: ga_dst.at[k])
    s_gb = family(8, lambda k: (gb_src.at[z_at(k)], gb_dst.at[k], z_peer(k)), lambda k: gb_dst.at[k])
    s_ml = family(4, lambda k: (ml_src.at[yl_at(k)], ml_dst.at[k], yl_peer(k)), lambda k: ml_dst.at[k])
    s_fc = family(2, lambda xb: (fc_src.at[xb], fc_dst.at[xb], sibling), lambda xb: fc_dst.at[xb])
    s_fx = family(4, lambda k: (fx_src.at[x_at(k)], fx_dst.at[k], x_peer(k)), lambda k: fx_dst.at[k])
    ff_send = bases[0]
    bases[0] += 2

    def ff(xb, h):
        return pltpu.make_async_remote_copy(
            src_ref=ff_src.at[xb],
            dst_ref=ff_dst.at[h],
            send_sem=send_sem.at[ff_send + xb],
            recv_sem=recv_sem.at[ff_send + h],
            device_id=(last_dp, last_t(xb)),
            device_id_type=MESH,
        )

    assert bases[0] <= SEMS

    own = [
        pltpu.make_async_copy(src, dst, own_sem.at[i])
        for i, (src, dst) in enumerate(
            ((cot, cot_g.at[yl]), (b, b_g.at[z]), (a, a_g.at[z]), (w, w_g.at[z]), (hid, hid_g.at[yl]))
        )
    ]
    for copy in own:
        copy.start()

    barrier = pltpu.get_barrier_semaphore()

    def greet(dev):
        pl.semaphore_signal(barrier, inc=1, device_id=dev, device_id_type=MESH)

    loop(3, lambda k: greet(yl_peer(k)))
    loop(7, lambda k: greet(z_peer(k)))
    loop(7, lambda k: greet(o_peer(k)))
    greet(partner)
    for xb in range(2):
        @pl.when(jnp.logical_not(last_here(xb)))
        def _(xb=xb):
            greet((last_dp, last_t(xb)))

        @pl.when(jnp.logical_not(first_here(xb)))
        def _(xb=xb):
            greet((first_dp, first_t(xb)))

    own_last = jnp.logical_or(last_here(0), last_here(1)).astype(jnp.int32)
    greet((far_row, lax.rem(t + 8, 16)))

    @pl.when(far_root)
    def _():
        loop(4, lambda row: greet((row * 8 + z, lax.rem(t + 8, 16))), 0)

    row = lax.broadcasted_iota(jnp.int32, (16, 128), 0)
    job = jnp.where(row < 8, block_job[0, 0], block_job[1, 0])
    for j in range(JOBS):
        lim[j] = jnp.where(job == j, ranks[j], 0).astype(F32)
    lim_g[yl] = lim[yl]

    for copy in own:
        copy.wait()
    pl.semaphore_wait(barrier, 23 - 2 * own_last + 4 * far_root.astype(jnp.int32))

    loop(3, s_cot.start)
    cry(yl).start()
    loop(3, s_lim.start)
    ring_pass(0)
    loop(7, s_b.start)
    loop(3, s_cot.landed)

    @pl.when(native_root)
    def _():
        cr[mine] = cot_g[...]
        loop(3, lambda k: crx(k, xb_me).start())

    loop(3, s_hid[0].start)
    loop(7, s_b.landed)

    def partial(i, value):
        part[i] = value.astype(BF).reshape(8, 64, 256)
        loop(7, s_part[i].start)

    def halfway(i):
        loop(7, s_part[i].landed)
        value = part[i, o].astype(F32)
        for k in range(1, 8):
            value = value + part_in[i, k].astype(F32)
        limit = lim_g[x, pl.ds(pl.multiple_of(c * 8, 8), 8), :][0:1, :]
        limit = jnp.concatenate([limit, limit], axis=1)
        column = lax.broadcasted_iota(jnp.int32, (64, 256), 1).astype(F32)
        value = jnp.where(column < limit, value, 0.0)
        tot[i] = value
        yh_out[i] = value.astype(BF)
        s_yh[i].start(0)

    def whole(i):
        s_yh[i].landed(0)
        low[i, o] = (tot[i] + yh_in[i].astype(F32)).astype(BF)
        loop(7, s_low[i].start)

    factor_b = b_g[...].reshape(256, 256)
    partial(0, dot(cot_g[...].reshape(512, 256), factor_b, NT))

    @pl.when(far_root)
    def _():
        for row in range(4):
            cry(row).wait_recv()
        loop(3, lambda k: crx(k, xb_me).start())

    ring_pass(1)
    loop(3, s_lim.landed)
    halfway(0)
    loop(3, s_hid[1].start)
    ring_pass(2)
    whole(0)
    ring_pass(3)

    for xb in range(2):
        @pl.when(x != lax.rem(yl, 2) * 2 + xb)
        def _(xb=xb):
            crx(1, xb).wait_recv()

        s_crc.start(xb)

    for half in s_hid:
        loop(3, half.landed)
    ring_pass(4)
    partial(1, dot(hid_g[...].reshape(512, 1024), a_g[...].reshape(256, 1024), NT))

    loop(7, s_low[0].landed)
    for xb in range(2):
        s_crc.landed(xb)

    def hg_tile(n):
        rows = slice(256 * n, 256 * (n + 1))
        acc = adapter_scale * dot(low[0].reshape(512, 256), a_g[:, :, rows].reshape(256, 256))
        for j in range(4):
            pair = jnp.concatenate([w_g[2 * j, rows, :], w_g[2 * j + 1, rows, :]], axis=1)
            acc = acc + dot(cr[j].reshape(512, 256), pair, NT)
        hg_src[n] = acc.astype(BF).reshape(4, 128, 256)
        loop(3, s_hg[n].start)

    def frozen(xb, cc):
        j = xb * 2 + cc
        pair = jnp.concatenate([w_g[2 * j], w_g[2 * j + 1]], axis=1)
        return dot(hid_g[...].reshape(512, 1024), pair)

    hg_tile(0)
    hg_tile(1)
    for xb in range(2):
        fc_src[xb] = frozen(xb, 1 - c).astype(BF)
        s_fc.start(xb)

    halfway(1)
    hg_tile(2)
    for xb in range(2):
        acc = frozen(xb, c)
        s_fc.landed(xb)
        acc = acc + fc_dst[xb].astype(F32)
        fx_src[:, xb] = acc.astype(BF).reshape(4, 128, 256)
    loop(3, s_fx.start)

    whole(1)
    hg_tile(3)

    for n in range(4):
        cols = slice(256 * n, 256 * (n + 1))
        term = adapter_scale * dot(low[0].reshape(512, 256), hid_g[:, :, cols].reshape(512, 256), TN)
        ga_src[:, :, cols] = term.astype(BF).reshape(8, 32, 256)
    loop(7, s_ga.start)

    loop(7, s_low[1].landed)
    ml_src[...] = (adapter_scale * dot(low[1].reshape(512, 256), factor_b)).astype(BF).reshape(4, 128, 256)
    loop(3, s_ml.start)
    gb_src[...] = (
        adapter_scale * dot(low[1].reshape(512, 256), cot_g[...].reshape(512, 256), TN)
    ).astype(BF).reshape(8, 32, 256)
    loop(7, s_gb.start)

    loop(3, s_fx.landed)
    value = fx_src[x].astype(F32)
    for k in range(1, 4):
        value = value + fx_dst[k].astype(F32)
    ff_src[...] = value.astype(BF)
    for xb in range(2):
        @pl.when(last_here(xb))
        def _(xb=xb):
            ff_dst[yh] = ff_src[xb]

        @pl.when(jnp.logical_not(last_here(xb)))
        def _(xb=xb):
            ff(xb, yh).start()

    for n in range(4):
        loop(3, s_hg[n].landed)
        value = hg_src[n, yl].astype(F32)
        for k in range(1, 4):
            value = value + hg_dst[n, k].astype(F32)
        hg_o[:, 256 * n : 256 * (n + 1)] = value.astype(BF)

    loop(7, s_ga.landed)
    value = ga_src[z].astype(F32)
    for k in range(1, 8):
        value = value + ga_dst[k].astype(F32)
    ga_o[...] = value.astype(BF)

    loop(7, s_gb.landed)
    value = gb_src[z].astype(F32)
    for k in range(1, 8):
        value = value + gb_dst[k].astype(F32)
    gb_o[...] = value.astype(BF)

    loop(3, s_ml.landed)
    for h in range(2):
        @pl.when(jnp.logical_not(first_here(h)))
        def _(h=h):
            ff(0, h).wait_recv()

    value = ff_dst[0].astype(F32) + ff_dst[1].astype(F32) + ml_src[yl].astype(F32)
    for k in range(1, 4):
        value = value + ml_dst[k].astype(F32)
    mixed_o[...] = value.astype(BF)

    for family_of in (s_cot, s_lim, *s_hid, s_ml, s_fx, *s_hg):
        loop(3, family_of.left)
    for family_of in (s_b, *s_part, *s_low, s_ga, s_gb):
        loop(7, family_of.left)
    for right, left, across in rings:
        loop(3, right.left)
        loop(3, left.left)
        across.left(0)
    for family_of in s_yh:
        family_of.left(0)
    for xb in range(2):
        s_crc.left(xb)
        s_fc.left(xb)

        @pl.when(jnp.logical_not(last_here(xb)))
        def _(xb=xb):
            ff(xb, yh).wait_send()

    cry(yl).wait_send()

    @pl.when(is_root)
    def _():
        loop(3, lambda k: crx(k, xb_me).wait_send())


SEMS = 160


def on_device(hidden, down_weight, factor_a, factor_b, cotangent, block_job, ranks):
    def vmem(*shape, dtype=BF):
        return pltpu.VMEM(shape, dtype)

    shapes = ((128, 256), (128, 1024), (32, 1024), (32, 256))
    return pl.pallas_call(
        kernel,
        out_shape=tuple(jax.ShapeDtypeStruct(s, BF) for s in shapes),
        in_specs=[pl.BlockSpec(memory_space=pltpu.HBM)] * 5 + [pl.BlockSpec(memory_space=pltpu.SMEM)] * 2,
        out_specs=tuple(pl.BlockSpec(memory_space=pltpu.VMEM) for s in shapes),
        scratch_shapes=[
            vmem(4, 128, 1024), vmem(8, 1024, 128), vmem(8, 32, 1024), vmem(8, 32, 256),
            vmem(4, 128, 256), vmem(4, 16, 128, dtype=F32), vmem(4, 16, 128, dtype=F32), vmem(4, 4, 128, 256),
            vmem(2, 8, 64, 256), vmem(2, 8, 64, 256), vmem(2, 64, 256, dtype=F32),
            vmem(2, 64, 256), vmem(2, 64, 256), vmem(2, 8, 64, 256),
            vmem(4, 4, 128, 256), vmem(4, 4, 128, 256), vmem(8, 32, 1024), vmem(8, 32, 1024),
            vmem(8, 32, 256), vmem(8, 32, 256), vmem(4, 128, 256), vmem(4, 128, 256),
            vmem(2, 512, 256), vmem(2, 512, 256), vmem(4, 2, 128, 256), vmem(4, 2, 128, 256),
            vmem(2, 128, 256), vmem(2, 128, 256),
            pltpu.SemaphoreType.DMA((5,)), pltpu.SemaphoreType.DMA((SEMS,)), pltpu.SemaphoreType.DMA((SEMS,)),
        ],
        compiler_params=pltpu.CompilerParams(
            collective_id=0, has_side_effects=True, vmem_limit_bytes=54528 * 1024
        ),
        cost_estimate=pl.CostEstimate(flops=3_000_000_000, bytes_accessed=4_000_000, transcendentals=0),
    )(hidden, down_weight, factor_a, factor_b, cotangent, block_job, ranks)


def solution(mesh):
    in_specs = (
        P("dp", "tensor"),
        P("tensor", "dp"),
        P("dp", "tensor"),
        P("dp", "tensor"),
        P("dp", "tensor"),
        P("dp", None),
        P(),
    )
    out_specs = (P("dp", "tensor"), P("dp", "tensor"), P("dp", "tensor"), P("dp", "tensor"))
    return jax.shard_map(
        on_device, mesh=mesh, in_specs=in_specs, out_specs=out_specs, check_vma=False
    )
```

```python
import jax
import jax.numpy as jnp
from jax import lax
from jax.experimental import pallas as pl
from jax.experimental.pallas import tpu as pltpu
from jax.sharding import PartitionSpec as P

R = 256
JOBS = 4
BLOCK = 64
NYL, NZ, NX = 4, 8, 4

BF = jnp.bfloat16
F32 = jnp.float32
MESH = pl.DeviceIdType.MESH
NN = (((1,), (0,)), ((), ()))
NT = (((1,), (1,)), ((), ()))
TN = (((0,), (0,)), ((), ()))

adapter_scale = 2.0


def dot(first, second, dims=NN):
    return lax.dot_general(first, second, dims, preferred_element_type=F32)


def loop(count, body, start=1):
    def step(k, carry):
        body(k)
        return carry

    lax.fori_loop(start, start + count, step, 0)


class Sends:
    def __init__(self, sems, base, out, into):
        self.send, self.recv = sems
        self.base, self.out, self.into = base, out, into

    def copy(self, k):
        src, dst, dev = self.out(k)
        return pltpu.make_async_remote_copy(
            src_ref=src,
            dst_ref=dst,
            send_sem=self.send.at[self.base + k],
            recv_sem=self.recv.at[self.base + k],
            device_id=dev,
            device_id_type=MESH,
        )

    def start(self, k):
        self.copy(k).start()

    def landed(self, k):
        src, dst, dev = self.out(k)
        pltpu.make_async_remote_copy(
            src_ref=src,
            dst_ref=self.into(k),
            send_sem=self.send.at[self.base + k],
            recv_sem=self.recv.at[self.base + k],
            device_id=dev,
            device_id_type=MESH,
        ).wait_recv()

    def left(self, k):
        self.copy(k).wait_send()


def kernel(
    hid, w, a, b, cot, block_job, ranks,
    mixed_o, hg_o, ga_o, gb_o,
    hid_g, w_g, a_g, b_g, cot_g, lim, lim_g, cr,
    part, part_in, tot, yh_out, yh_in, low,
    hg_src, hg_far, hg_sum, hg_dst, ga_src, ga_dst, gb_src, gb_dst, ml_src, ml_dst,
    fc_src, fc_dst, fx_src, fx_dst, ff_src, ff_dst,
    own_sem, send_sem, recv_sem,
):
    d = lax.axis_index("dp")
    t = lax.axis_index("tensor")
    yl, z = lax.div(d, 8), lax.rem(d, 8)
    yh, o = lax.div(t, 8), lax.rem(t, 8)
    x, c = lax.div(o, 2), lax.rem(o, 2)

    def yl_at(k):
        return lax.rem(yl + k + 4, 4)

    def z_at(k):
        return lax.rem(z + k + 16, 8)

    def o_at(k):
        return lax.rem(o + k + 8, 8)

    def x_at(k):
        return lax.rem(x + k + 4, 4)

    def yl_peer(k):
        return (yl_at(k) * 8 + z, t)

    def z_peer(k):
        return (yl * 8 + z_at(k), t)

    def o_peer(k):
        return (d, yh * 8 + o_at(k))

    def x_peer(k):
        return (d, yh * 8 + x_at(k) * 2 + c)

    sibling = (d, t + 1 - 2 * c)
    partner = (d, lax.rem(t + 8, 16))

    last_dp = x * 8 + z

    def last_t(xb):
        return lax.div(yl, 2) * 8 + (lax.rem(yl, 2) * 2 + xb) * 2 + c

    def last_here(xb):
        return jnp.logical_and(last_dp == d, last_t(xb) == t)

    first_dp = (2 * yh + lax.div(x, 2)) * 8 + z

    def first_t(h):
        return h * 8 + yl * 2 + c

    def first_here(h):
        return jnp.logical_and(first_dp == d, first_t(h) == t)

    sems = (send_sem, recv_sem)
    bases = [0]

    def family(count, out, into):
        base = bases[0]
        bases[0] += count
        return Sends(sems, base, out, into)

    s_cot = family(4, lambda k: (cot_g.at[yl], cot_g.at[yl], yl_peer(k)), lambda k: cot_g.at[yl_at(-k)])
    s_lim = family(4, lambda k: (lim.at[yl_at(k)], lim_g.at[yl], yl_peer(k)), lambda k: lim_g.at[yl_at(-k)])
    s_hid = [
        family(
            4,
            lambda k, h=h: (hid_g.at[yl, h], hid_g.at[yl, h], yl_peer(k)),
            lambda k, h=h: hid_g.at[yl_at(-k), h],
        )
        for h in (pl.ds(0, 64), pl.ds(64, 64))
    ]
    s_b = family(8, lambda k: (b_g.at[z], b_g.at[z], z_peer(k)), lambda k: b_g.at[z_at(-k)])
    turn = 1 - 2 * c
    rings = []
    for at in (
        lambda slot: a_g.at[slot],
        lambda slot: w_g.at[slot, pl.ds(0, 512)],
        lambda slot: w_g.at[slot, pl.ds(512, 512)],
    ):
        right = family(
            4,
            lambda s, at=at: (at(z_at(1 - s)), at(z_at(1 - s)), z_peer(1)),
            lambda s, at=at: at(z_at(-s)),
        )
        left = family(
            4,
            lambda s, at=at: (at(z_at(s - 1)), at(z_at(s - 1)), z_peer(-1)),
            lambda s, at=at: at(z_at(s)),
        )
        across = family(
            1,
            lambda s, at=at: (at(z_at(-3 * turn)), at(z_at(-3 * turn)), z_peer(turn)),
            lambda s, at=at: at(z_at(4)),
        )
        rings.append((right, left, across))

    def ring_pass(s):
        for right, left, across in rings:
            if s == 4:
                across.landed(0)
                continue
            if s > 0:
                right.landed(s)
                left.landed(s)
            if s < 3:
                right.start(s + 1)
                left.start(s + 1)
            else:
                across.start(0)

    s_part, s_yh, s_low = [], [], []
    for i in range(2):
        s_part.append(
            family(8, lambda k, i=i: (part.at[i, o_at(k)], part_in.at[i, k], o_peer(k)), lambda k, i=i: part_in.at[i, k])
        )
        s_yh.append(family(1, lambda k, i=i: (yh_out.at[i], yh_in.at[i], partner), lambda k, i=i: yh_in.at[i]))
        s_low.append(
            family(8, lambda k, i=i: (low.at[i, o], low.at[i, o], o_peer(k)), lambda k, i=i: low.at[i, o_at(-k)])
        )

    odd = lax.rem(x, 2)
    is_root = lax.div(x, 2) == lax.rem(yl, 2)
    is_native = yh == lax.div(yl, 2)
    native_root = jnp.logical_and(is_root, is_native)
    far_root = jnp.logical_and(is_root, jnp.logical_not(is_native))
    root_piece = odd * 2 + c
    nearer = jnp.where(is_root, odd, 1 - odd)
    piece, other_piece = nearer * 2 + c, (1 - nearer) * 2 + c
    far_row = (2 * yh + lax.div(x, 2)) * 8 + z
    cry_base = bases[0]
    bases[0] += 4

    def cry(row):
        return pltpu.make_async_remote_copy(
            src_ref=cot_g.at[yl],
            dst_ref=cr.at[root_piece, row],
            send_sem=send_sem.at[cry_base],
            recv_sem=recv_sem.at[cry_base + row],
            device_id=(far_row, lax.rem(t + 8, 16)),
            device_id_type=MESH,
        )

    s_out = family(
        4, lambda row: (cr.at[piece, row], cr.at[piece, row], x_peer(2 * odd - 1)), lambda row: cr.at[piece, row]
    )
    s_over = family(
        4, lambda row: (cr.at[piece, row], cr.at[piece, row], x_peer(1 - 2 * odd)), lambda row: cr.at[other_piece, row]
    )
    s_crc = family(2, lambda xb: (cr.at[xb * 2 + c], cr.at[xb * 2 + c], sibling), lambda xb: cr.at[xb * 2 + 1 - c])

    side = lax.div(yl, 2)
    mate_row = yl + 1 - 2 * lax.rem(yl, 2)
    mate = (mate_row * 8 + z, t)
    at_edge = lax.rem(yl, 2) == side
    at_middle = jnp.logical_not(at_edge)

    def other_row(q):
        return 2 - side if q == 0 else 3 * (1 - side)

    s_hg_near = family(4, lambda n: (hg_src.at[n, mate_row], hg_dst.at[n, 0], mate), lambda n: hg_dst.at[n, 0])
    s_hg_far = []
    for q in range(2):
        s_hg_far.append(
            family(4, lambda n, q=q: (hg_src.at[n, other_row(q)], hg_far.at[n, q], mate), lambda n, q=q: hg_far.at[n, q])
        )
    hg_sum_send = bases[0]
    bases[0] += 8

    def hg_total(n, q):
        return pltpu.make_async_remote_copy(
            src_ref=hg_sum.at[n, q],
            dst_ref=hg_dst.at[n, 1],
            send_sem=send_sem.at[hg_sum_send + 4 * q + n],
            recv_sem=recv_sem.at[hg_sum_send + n],
            device_id=(other_row(q) * 8 + z, t),
            device_id_type=MESH,
        )

    s_ga = family(8, lambda k: (ga_src.at[z_at(k)], ga_dst.at[k], z_peer(k)), lambda k: ga_dst.at[k])
    s_gb = family(8, lambda k: (gb_src.at[z_at(k)], gb_dst.at[k], z_peer(k)), lambda k: gb_dst.at[k])
    s_ml = family(4, lambda k: (ml_src.at[yl_at(k)], ml_dst.at[k], yl_peer(k)), lambda k: ml_dst.at[k])
    s_fc = family(2, lambda xb: (fc_src.at[xb], fc_dst.at[xb], sibling), lambda xb: fc_dst.at[xb])
    s_fx = family(4, lambda k: (fx_src.at[x_at(k)], fx_dst.at[k], x_peer(k)), lambda k: fx_dst.at[k])
    ff_send = bases[0]
    bases[0] += 2

    def ff(xb, h):
        return pltpu.make_async_remote_copy(
            src_ref=ff_src.at[xb],
            dst_ref=ff_dst.at[h],
            send_sem=send_sem.at[ff_send + xb],
            recv_sem=recv_sem.at[ff_send + h],
            device_id=(last_dp, last_t(xb)),
            device_id_type=MESH,
        )

    assert bases[0] <= SEMS

    own = [
        pltpu.make_async_copy(src, dst, own_sem.at[i])
        for i, (src, dst) in enumerate(
            ((cot, cot_g.at[yl]), (b, b_g.at[z]), (a, a_g.at[z]), (w, w_g.at[z]), (hid, hid_g.at[yl]))
        )
    ]
    for copy in own:
        copy.start()

    barrier = pltpu.get_barrier_semaphore()

    def greet(dev):
        pl.semaphore_signal(barrier, inc=1, device_id=dev, device_id_type=MESH)

    loop(3, lambda k: greet(yl_peer(k)))
    loop(7, lambda k: greet(z_peer(k)))
    loop(7, lambda k: greet(o_peer(k)))
    greet(partner)
    for xb in range(2):
        @pl.when(jnp.logical_not(last_here(xb)))
        def _(xb=xb):
            greet((last_dp, last_t(xb)))

        @pl.when(jnp.logical_not(first_here(xb)))
        def _(xb=xb):
            greet((first_dp, first_t(xb)))

    own_last = jnp.logical_or(last_here(0), last_here(1)).astype(jnp.int32)
    greet((far_row, lax.rem(t + 8, 16)))

    @pl.when(far_root)
    def _():
        loop(4, lambda row: greet((row * 8 + z, lax.rem(t + 8, 16))), 0)

    row = lax.broadcasted_iota(jnp.int32, (16, 128), 0)
    job = jnp.where(row < 8, block_job[0, 0], block_job[1, 0])
    for j in range(JOBS):
        lim[j] = jnp.where(job == j, ranks[j], 0).astype(F32)
    lim_g[yl] = lim[yl]

    for copy in own:
        copy.wait()
    pl.semaphore_wait(barrier, 23 - 2 * own_last + 4 * far_root.astype(jnp.int32))

    loop(3, s_cot.start)
    cry(yl).start()
    loop(3, s_lim.start)
    ring_pass(0)
    loop(7, s_b.start)
    loop(3, s_cot.landed)

    @pl.when(native_root)
    def _():
        cr[piece] = cot_g[...]
        for row in range(4):
            s_out.start(row)
            s_over.start(row)

    loop(3, s_hid[0].start)
    loop(7, s_b.landed)

    def partial(i, value):
        part[i] = value.astype(BF).reshape(8, 64, 256)
        loop(7, s_part[i].start)

    def halfway(i):
        loop(7, s_part[i].landed)
        value = part[i, o].astype(F32)
        for k in range(1, 8):
            value = value + part_in[i, k].astype(F32)
        limit = lim_g[x, pl.ds(pl.multiple_of(c * 8, 8), 8), :][0:1, :]
        limit = jnp.concatenate([limit, limit], axis=1)
        column = lax.broadcasted_iota(jnp.int32, (64, 256), 1).astype(F32)
        value = jnp.where(column < limit, value, 0.0)
        tot[i] = value
        yh_out[i] = value.astype(BF)
        s_yh[i].start(0)

    def whole(i):
        s_yh[i].landed(0)
        low[i, o] = (tot[i] + yh_in[i].astype(F32)).astype(BF)
        loop(7, s_low[i].start)

    factor_b = b_g[...].reshape(256, 256)
    partial(0, dot(cot_g[...].reshape(512, 256), factor_b, NT))

    @pl.when(far_root)
    def _():
        for row in range(4):
            cry(row).wait_recv()
            s_out.start(row)
            s_over.start(row)

    ring_pass(1)
    loop(3, s_lim.landed)
    halfway(0)
    loop(3, s_hid[1].start)
    @pl.when(jnp.logical_not(is_root))
    def _():
        for row in range(4):
            s_out.landed(row)
            s_over.start(row)

    ring_pass(2)
    whole(0)
    s_crc.start(nearer)
    ring_pass(3)
    loop(4, s_over.landed, 0)
    s_crc.start(1 - nearer)

    for half in s_hid:
        loop(3, half.landed)
    ring_pass(4)
    partial(1, dot(hid_g[...].reshape(512, 1024), a_g[...].reshape(256, 1024), NT))

    loop(7, s_low[0].landed)
    for xb in range(2):
        s_crc.landed(xb)

    def hg_tile(n):
        rows = slice(256 * n, 256 * (n + 1))
        acc = adapter_scale * dot(low[0].reshape(512, 256), a_g[:, :, rows].reshape(256, 256))
        for j in range(4):
            pair = jnp.concatenate([w_g[2 * j, rows, :], w_g[2 * j + 1, rows, :]], axis=1)
            acc = acc + dot(cr[j].reshape(512, 256), pair, NT)
        hg_src[n] = acc.astype(BF).reshape(4, 128, 256)

        @pl.when(at_edge)
        def _():
            s_hg_far[1].start(n)
            s_hg_far[0].start(n)

        s_hg_near.start(n)

    def hg_middle(n):
        @pl.when(at_middle)
        def _():
            for q in (1, 0):
                s_hg_far[q].landed(n)
                own_term = hg_src[n, other_row(q)].astype(F32)
                hg_sum[n, q] = (own_term + hg_far[n, q].astype(F32)).astype(BF)
                hg_total(n, q).start()

    def frozen(xb, cc):
        j = xb * 2 + cc
        pair = jnp.concatenate([w_g[2 * j], w_g[2 * j + 1]], axis=1)
        return dot(hid_g[...].reshape(512, 1024), pair)

    hg_tile(0)
    hg_tile(1)
    for xb in range(2):
        fc_src[xb] = frozen(xb, 1 - c).astype(BF)
        s_fc.start(xb)

    for n in range(4):
        cols = slice(256 * n, 256 * (n + 1))
        term = adapter_scale * dot(low[0].reshape(512, 256), hid_g[:, :, cols].reshape(512, 256), TN)
        ga_src[:, :, cols] = term.astype(BF).reshape(8, 32, 256)
    loop(7, s_ga.start)

    halfway(1)
    hg_middle(0)
    hg_tile(2)
    for xb in range(2):
        acc = frozen(xb, c)
        s_fc.landed(xb)
        acc = acc + fc_dst[xb].astype(F32)
        fx_src[:, xb] = acc.astype(BF).reshape(4, 128, 256)
    loop(3, s_fx.start)

    hg_middle(1)
    hg_tile(3)
    whole(1)
    hg_middle(2)
    loop(3, s_fx.landed)
    value = fx_src[x].astype(F32)
    for k in range(1, 4):
        value = value + fx_dst[k].astype(F32)
    ff_src[...] = value.astype(BF)
    for xb in range(2):
        @pl.when(last_here(xb))
        def _(xb=xb):
            ff_dst[yh] = ff_src[xb]

        @pl.when(jnp.logical_not(last_here(xb)))
        def _(xb=xb):
            ff(xb, yh).start()

    hg_middle(3)
    loop(7, s_low[1].landed)
    gb_src[...] = (
        adapter_scale * dot(low[1].reshape(512, 256), cot_g[...].reshape(512, 256), TN)
    ).astype(BF).reshape(8, 32, 256)
    loop(7, s_gb.start)

    ml_src[...] = (adapter_scale * dot(low[1].reshape(512, 256), factor_b)).astype(BF).reshape(4, 128, 256)
    loop(3, s_ml.start)

    for n in range(4):
        s_hg_near.landed(n)
        hg_total(n, 0).wait_recv()
        value = hg_src[n, yl].astype(F32) + hg_dst[n, 0].astype(F32) + hg_dst[n, 1].astype(F32)
        hg_o[:, 256 * n : 256 * (n + 1)] = value.astype(BF)

    loop(7, s_ga.landed)
    value = ga_src[z].astype(F32)
    for k in range(1, 8):
        value = value + ga_dst[k].astype(F32)
    ga_o[...] = value.astype(BF)

    loop(7, s_gb.landed)
    value = gb_src[z].astype(F32)
    for k in range(1, 8):
        value = value + gb_dst[k].astype(F32)
    gb_o[...] = value.astype(BF)

    loop(3, s_ml.landed)
    for h in range(2):
        @pl.when(jnp.logical_not(first_here(h)))
        def _(h=h):
            ff(0, h).wait_recv()

    value = ff_dst[0].astype(F32) + ff_dst[1].astype(F32) + ml_src[yl].astype(F32)
    for k in range(1, 4):
        value = value + ml_dst[k].astype(F32)
    mixed_o[...] = value.astype(BF)

    for family_of in (s_cot, s_lim, *s_hid, s_ml, s_fx):
        loop(3, family_of.left)
    for family_of in (s_b, *s_part, *s_low, s_ga, s_gb):
        loop(7, family_of.left)
    for right, left, across in rings:
        loop(3, right.left)
        loop(3, left.left)
        across.left(0)
    for family_of in s_yh:
        family_of.left(0)
    for xb in range(2):
        s_crc.left(xb)
        s_fc.left(xb)

        @pl.when(jnp.logical_not(last_here(xb)))
        def _(xb=xb):
            ff(xb, yh).wait_send()

    cry(yl).wait_send()
    loop(4, s_hg_near.left, 0)

    @pl.when(at_edge)
    def _():
        for q in range(2):
            loop(4, s_hg_far[q].left, 0)

    @pl.when(at_middle)
    def _():
        for n in range(4):
            for q in range(2):
                hg_total(n, q).wait_send()

    loop(4, s_over.left, 0)

    @pl.when(is_root)
    def _():
        loop(4, s_out.left, 0)


SEMS = 160


def on_device(hidden, down_weight, factor_a, factor_b, cotangent, block_job, ranks):
    def vmem(*shape, dtype=BF):
        return pltpu.VMEM(shape, dtype)

    shapes = ((128, 256), (128, 1024), (32, 1024), (32, 256))
    return pl.pallas_call(
        kernel,
        out_shape=tuple(jax.ShapeDtypeStruct(s, BF) for s in shapes),
        in_specs=[pl.BlockSpec(memory_space=pltpu.HBM)] * 5 + [pl.BlockSpec(memory_space=pltpu.SMEM)] * 2,
        out_specs=tuple(pl.BlockSpec(memory_space=pltpu.VMEM) for s in shapes),
        scratch_shapes=[
            vmem(4, 128, 1024), vmem(8, 1024, 128), vmem(8, 32, 1024), vmem(8, 32, 256),
            vmem(4, 128, 256), vmem(4, 16, 128, dtype=F32), vmem(4, 16, 128, dtype=F32), vmem(4, 4, 128, 256),
            vmem(2, 8, 64, 256), vmem(2, 8, 64, 256), vmem(2, 64, 256, dtype=F32),
            vmem(2, 64, 256), vmem(2, 64, 256), vmem(2, 8, 64, 256),
            vmem(4, 4, 128, 256), vmem(4, 2, 128, 256), vmem(4, 2, 128, 256), vmem(4, 2, 128, 256),
            vmem(8, 32, 1024), vmem(8, 32, 1024),
            vmem(8, 32, 256), vmem(8, 32, 256), vmem(4, 128, 256), vmem(4, 128, 256),
            vmem(2, 512, 256), vmem(2, 512, 256), vmem(4, 2, 128, 256), vmem(4, 2, 128, 256),
            vmem(2, 128, 256), vmem(2, 128, 256),
            pltpu.SemaphoreType.DMA((5,)), pltpu.SemaphoreType.DMA((SEMS,)), pltpu.SemaphoreType.DMA((SEMS,)),
        ],
        compiler_params=pltpu.CompilerParams(
            collective_id=0, has_side_effects=True, vmem_limit_bytes=54528 * 1024
        ),
        cost_estimate=pl.CostEstimate(flops=3_000_000_000, bytes_accessed=4_000_000, transcendentals=0),
    )(hidden, down_weight, factor_a, factor_b, cotangent, block_job, ranks)


def solution(mesh):
    in_specs = (
        P("dp", "tensor"),
        P("tensor", "dp"),
        P("dp", "tensor"),
        P("dp", "tensor"),
        P("dp", "tensor"),
        P("dp", None),
        P(),
    )
    out_specs = (P("dp", "tensor"), P("dp", "tensor"), P("dp", "tensor"), P("dp", "tensor"))
    return jax.shard_map(
        on_device, mesh=mesh, in_specs=in_specs, out_specs=out_specs, check_vma=False
    )
```
